256 devices in a mesh: vocab: 8 (over x, z_lo), tok: 32 (over z_hi, y, core).
Axes of the slice: x: 4, y: 4, z: 8 (z_hi: 4, z_lo: 2; z = z_hi * 2 + z_lo), core: 2. Of those that a mesh axis runs over, the one named last changes fastest.
Arguments:
- hidden: bfloat16 [16384, 5376], P('tok', 'vocab'), may hold values from -2 to 2
- head_weight: bfloat16 [6144, 5376], P('vocab'), may hold values from -4 to 4
- targets: int32 [16384], P('tok'), may hold values from 0 to 6143
- loss_grad: float32 [16384], P('tok'), may hold values from 1 to 10
Outputs:
- input_grad: bfloat16 [16384, 5376], P('tok', 'vocab')
- head_grad: float32 [6144, 5376], P(('vocab', 'tok'))
- token_loss: float32 [16384], P('tok')
The draws below stay inside these ranges and needn't reach their ends.
All inputs are finite; a program needn't handle non-finite values.
Results may differ from the reference program's by a relative error of at most 0.005.
Values may be sent and summed in bfloat16 or wider, within the bound.
A program may use at most 128 MiB of HBM per device.

```python
import math
import jax
import jax.numpy as jnp
from jax import lax

D = 5376
VOC_DEV = 768
TOK_DEV = 512
VOCAB = 6144
TOKENS = 16384


strengths = (120.0, 200.0, 300.0, 420.0)


def shared_signs(key):
    return jax.random.rademacher(key, (4, D), dtype=jnp.float32)


def strong_tokens():
    return [number * (TOKENS // 4) + 5 for number in range(4)]


def strong_vocab(number):
    first_row = number * (VOCAB // 4) + 3
    return (first_row, (first_row + VOC_DEV + 7) % VOCAB)


def amplitude(number):
    return math.sqrt(strengths[number] / (2.0 * D))


def draw_hidden(key, part):
    signs = shared_signs(key)
    key = jax.random.fold_in(key, 11)
    values = jnp.clip(jax.random.normal(key, (TOKENS, D), jnp.float32), -4.0, 4.0) * 0.15
    for number, token_row in enumerate(strong_tokens()):
        values = values.at[token_row].set(amplitude(number) * signs[number])
    return values.astype(jnp.bfloat16)


def draw_head_weight(key, part):
    signs = shared_signs(key)
    key = jax.random.fold_in(key, 12)
    values = jnp.clip(jax.random.normal(key, (VOCAB, D), jnp.float32), -4.0, 4.0) * 0.27
    for number in range(4):
        first_row, second_row = strong_vocab(number)
        row_values = 2.0 * amplitude(number) * signs[number]
        values = values.at[first_row].set(row_values)
        values = values.at[second_row].set(row_values * (1.0 - 2.0 / strengths[number]))
    return values.astype(jnp.bfloat16)


def plant(array, rng, least, top_value):
    spot = [jax.random.randint(jax.random.fold_in(rng, axis), (), 0, length) for axis, length in enumerate(array.shape)]
    main_axis = array.shape.index(max(array.shape))
    neighbour = spot[:main_axis] + [(spot[main_axis] + 1) % array.shape[main_axis]] + spot[main_axis + 1:]
    return array.at[tuple(spot)].set(least).at[tuple(neighbour)].set(top_value)


def steps_of(rng, dims, pieces, least, largest):
    loudness, own = 1.0, jax.random.fold_in(rng, 6)
    for axis_at, shards_of in pieces:
        heights = jnp.exp(jax.random.uniform(jax.random.fold_in(own, axis_at), (shards_of,), jnp.float32, least / len(pieces), largest / len(pieces)))
        loudness = loudness * jnp.repeat(heights, dims[axis_at] // shards_of).reshape([-1 if axis == axis_at else 1 for axis in range(len(dims))])
    return loudness


def setup_inputs(seed: int = 0) -> dict:
    key_of = jax.random.split(jax.random.key(seed), 5)
    hidden = draw_hidden(jax.random.fold_in(key_of[4], 71), 0)
    head_weight = draw_head_weight(jax.random.fold_in(key_of[4], 71), 0)
    targets = plant(jax.random.randint(key_of[2], (TOKENS,), 0, VOCAB), jax.random.fold_in(key_of[2], 1), 0, VOCAB - 1).astype(jnp.int32)
    loss_grad = jnp.clip(jnp.exp(math.log(10.0) - 2.3025851 * jax.random.uniform(key_of[3], (TOKENS,), jnp.float32) ** steps_of(key_of[3], (TOKENS,), ((0, 32),), -0.2, 0.2)), 1.0, 10.0)
    return dict(hidden=hidden, head_weight=head_weight, targets=targets, loss_grad=loss_grad)


def reference(hidden, head_weight, targets, loss_grad):
    vocab_ids = jnp.arange(VOCAB, dtype=jnp.int32)
    blocks = TOKENS // TOK_DEV

    def advance(accum_grad, inputs):
        rows_in, wanted, scales = inputs
        logits = jnp.dot(rows_in, head_weight.T, preferred_element_type=jnp.float32)
        row_peak = jnp.max(logits, axis=1)
        row_total = jnp.sum(jnp.exp(logits - row_peak[:, None]), axis=1)
        log_total = row_peak + jnp.log(row_total)
        matches = vocab_ids[None, :] == wanted[:, None]
        target_logit = jnp.sum(jnp.where(matches, logits, 0.0), axis=1)
        probability = jnp.exp(logits - log_total[:, None])
        dlogits = (scales[:, None] * (probability - matches.astype(jnp.float32))).astype(jnp.bfloat16)
        input_rows = jnp.dot(dlogits, head_weight, preferred_element_type=jnp.float32).astype(jnp.bfloat16)
        accum_grad = accum_grad + lax.dot_general(dlogits, rows_in, (((0,), (0,)), ((), ())), preferred_element_type=jnp.float32)
        return accum_grad, (input_rows, log_total - target_logit)

    initial = jnp.zeros((VOCAB, D), jnp.float32)
    head_grad, outputs = lax.scan(advance, initial, (hidden.reshape(blocks, TOK_DEV, D), targets.reshape(blocks, TOK_DEV), loss_grad.reshape(blocks, TOK_DEV)))
    input_grad, token_loss = outputs
    return input_grad.reshape(TOKENS, D), head_grad, token_loss.reshape(TOKENS)
```

```python
import jax
import jax.numpy as jnp
from jax import lax
from jax.experimental import pallas as pl
from jax.experimental.pallas import tpu as pltpu
from jax.sharding import PartitionSpec as P

MESH = pl.DeviceIdType.MESH
D = 5376
VOC = 768
TOK = 512
COL = 672
HALF = COL // 2
CUT = 560
CHUNKS = 3
WIDE = D // 2 // CHUNKS
GROUP = 48
BF = jnp.bfloat16
F32 = jnp.float32


def rows(start, size):
    return pl.ds(pl.multiple_of(start, 16), size)


def body(
    hidden, weight, targets, scales, grad_in, grad_head, loss,
    staged, weight_t, held, held_other, logits, dlog, dlog_other, stats,
    b_out, b_in, b_zout, b_zin, g_sum, c_out, c_in, c_zout, c_zin, last_out, last_in,
    local_sem, send_sem, recv_sem,
):
    vocab = lax.axis_index("vocab")
    tok = lax.axis_index("tok")
    x, z_lo = vocab // 2, vocab % 2
    core, y, z_hi = tok % 2, (tok // 2) % 4, tok // 8

    def in_vocab(dx, dz):
        return ((x + dx) % 4) * 2 + (z_lo + dz) % 2

    def in_tok(dz, dy, dc):
        return (((z_hi + dz) % 4) * 4 + (y + dy) % 4) * 2 + (core + dc) % 2

    def at_vocab(dx, dz):
        return (in_vocab(dx, dz), tok)

    def at_tok(dz, dy, dc):
        return (vocab, in_tok(dz, dy, dc))

    peers = [at_vocab(dx, dz) for dx in range(4) for dz in range(2) if dx or dz]
    others = [at_tok(0, 0, 1), at_tok(0, 1, 0), at_tok(0, 3, 0)]
    others += [at_tok(dz, 0, 0) for dz in (1, 2, 3)]

    barrier = pltpu.get_barrier_semaphore()
    for device in peers + others:
        pl.semaphore_signal(barrier, inc=1, device_id=device, device_id_type=MESH)

    fetch = pltpu.make_async_copy(weight, staged, local_sem)
    fetch.start()

    started = []

    def send(src, dst, device):
        at = len(started)
        copy = pltpu.make_async_remote_copy(
            src_ref=src,
            dst_ref=dst,
            send_sem=send_sem.at[at],
            recv_sem=recv_sem.at[at],
            device_id=device,
            device_id_type=MESH,
        )
        copy.start()
        started.append(copy)
        return copy

    def piece(block, start, stop):
        return held.at[rows(block * COL + start, stop - start)]

    def pass_on(block, start, stop, device):
        return send(piece(block, start, stop), piece(block, start, stop), device)

    right, left, pair = at_vocab(1, 0), at_vocab(3, 0), at_vocab(0, 1)
    own = vocab
    held[rows(own * COL, COL), :] = hidden[...].T
    pl.semaphore_wait(barrier, len(peers) + len(others))

    own_right_a = pass_on(own, 0, HALF, right)
    own_left_b = pass_on(own, HALF, COL, left)
    own_pair_a = pass_on(own, 0, HALF, pair)
    own_right_b = pass_on(own, HALF, COL, right)
    own_left_a = pass_on(own, 0, HALF, left)
    own_pair_b = pass_on(own, HALF, COL, pair)

    def turn(first, count):
        def step(i, _):
            at = pl.multiple_of((first + i) * 128, 128)
            weight_t[pl.ds(at, 128), :] = staged[:, pl.ds(at, 128)].T
            return 0

        lax.fori_loop(0, count, step, 0)

    def logit_part(block, fresh=False):
        def step(i, _):
            at = pl.multiple_of(i * 256, 256)
            part = lax.dot_general(
                weight_t[rows(block * COL, COL), pl.ds(at, 256)],
                held[rows(block * COL, COL), :],
                (((0,), (0,)), ((), ())),
                preferred_element_type=F32,
            )
            if fresh:
                logits[pl.ds(at, 256), :] = part
            else:
                logits[pl.ds(at, 256), :] += part
            return 0

        lax.fori_loop(0, VOC // 256, step, 0)

    fetch.wait()
    turn(0, 14)
    from_left, from_right = in_vocab(3, 0), in_vocab(1, 0)
    across, partner = in_vocab(2, 0), in_vocab(0, 1)
    own_right_a.wait_recv()
    on_right = pass_on(from_left, 0, HALF, right)
    own_left_b.wait_recv()
    on_left = pass_on(from_right, HALF, COL, left)
    turn(14, 14)
    own_pair_a.wait_recv()
    z_right_a = pass_on(partner, 0, HALF, right)
    z_left_a = pass_on(partner, 0, HALF, left)
    own_right_b.wait_recv()
    own_left_a.wait_recv()
    z_from_left = pass_on(from_left, CUT, COL, pair)
    z_from_right = pass_on(from_right, CUT, COL, pair)
    own_pair_b.wait_recv()
    z_right_b = pass_on(partner, HALF, CUT, right)
    z_left_b = pass_on(partner, HALF, CUT, left)
    turn(28, 14)
    on_right.wait_recv()
    z_across_a = pass_on(across, 0, HALF, pair)
    on_left.wait_recv()
    z_across_b = pass_on(across, HALF, COL, pair)
    logit_part(own, fresh=True)
    logit_part(from_left)
    logit_part(from_right)
    logit_part(partner)
    logit_part(across)
    z_from_left.wait_recv()
    z_right_a.wait_recv()
    z_right_b.wait_recv()
    logit_part(in_vocab(3, 1))
    z_from_right.wait_recv()
    z_left_a.wait_recv()
    z_left_b.wait_recv()
    logit_part(in_vocab(1, 1))
    z_across_a.wait_recv()
    z_across_b.wait_recv()
    share = send(
        held.at[rows((1 - core) * (D // 2), D // 2)], held_other, at_tok(0, 0, 1)
    )
    logit_part(in_vocab(2, 1))

    chosen = targets[...] - vocab * VOC
    steps = VOC // 64
    peak = jnp.full((8, TOK), -jnp.inf, F32)

    def find_peak(i, peak):
        part = logits[pl.ds(pl.multiple_of(i * 64, 64), 64), :]
        return jnp.maximum(peak, jnp.max(part.reshape(8, 8, TOK), axis=0))

    peak = lax.fori_loop(0, steps, find_peak, peak)
    peak = jnp.max(peak, axis=0, keepdims=True)
    ids = lax.broadcasted_iota(jnp.int32, (64, TOK), 0)

    def add_up(i, carry):
        total, picked = carry
        at = pl.multiple_of(i * 64, 64)
        part = logits[pl.ds(at, 64), :]
        hit = ids == chosen - at
        picked += jnp.sum(jnp.where(hit, part, 0.0).reshape(8, 8, TOK), axis=0)
        part = jnp.exp(part - peak)
        logits[pl.ds(at, 64), :] = part
        total += jnp.sum(part.reshape(8, 8, TOK), axis=0)
        return total, picked

    zeros = jnp.zeros((8, TOK), F32)
    total, picked = lax.fori_loop(0, steps, add_up, (zeros, zeros))
    total = jnp.sum(total, axis=0, keepdims=True)
    picked = jnp.sum(picked, axis=0, keepdims=True)
    stats[own] = jnp.concatenate([peak, total, picked, zeros[:5]], axis=0)
    told = [send(stats.at[own], stats.at[own], device) for device in peers]
    for copy in told:
        copy.wait_recv()
    heard = stats[...]
    peaks, totals, picks = heard[:, 0, :], heard[:, 1, :], heard[:, 2, :]
    row_peak = jnp.max(peaks, axis=0, keepdims=True)
    row_total = jnp.sum(totals * jnp.exp(peaks - row_peak), axis=0, keepdims=True)
    target_logit = jnp.sum(picks, axis=0, keepdims=True)
    loss[...] = row_peak + jnp.log(row_total) - target_logit
    share_of = jnp.exp(peak - row_peak) / row_total
    scale = scales[...]

    def make_dlog(i, _):
        at = pl.multiple_of(i * 64, 64)
        part = logits[pl.ds(at, 64), :] * share_of
        hit = ids == chosen - at
        part = scale * (part - jnp.where(hit, 1.0, 0.0))
        dlog[pl.ds(at, 64), :] = part.astype(BF)
        return 0

    lax.fori_loop(0, steps, make_dlog, 0)
    share_dlog = send(dlog, dlog_other, at_tok(0, 0, 1))

    def input_part(block, start):
        return jnp.dot(
            weight_t[rows(block * COL + start, HALF), :],
            dlog[...],
            preferred_element_type=F32,
        )

    def across_x(plane):
        block = in_vocab(2, plane)
        slots = b_out.at[plane], b_in.at[plane]
        slots[0][0] = input_part(block, 0).astype(BF)
        a = send(slots[0].at[0], slots[1].at[0], left)
        slots[0][1] = input_part(block, HALF).astype(BF)
        return a, send(slots[0].at[1], slots[1].at[1], right)

    def direct_x(plane):
        slots = b_out.at[plane], b_in.at[plane]
        slots[0][2] = input_part(in_vocab(3, plane), HALF).astype(BF)
        b = send(slots[0].at[2], slots[1].at[2], left)
        slots[0][3] = input_part(in_vocab(1, plane), 0).astype(BF)
        return b, send(slots[0].at[3], slots[1].at[3], right)

    def joined_x(plane, far):
        slots = b_out.at[plane], b_in.at[plane]
        far[0].wait_recv()
        part = input_part(in_vocab(3, plane), 0)
        slots[0][4] = (part + slots[1][0].astype(F32)).astype(BF)
        a = send(slots[0].at[4], slots[1].at[4], left)
        far[1].wait_recv()
        part = input_part(in_vocab(1, plane), HALF)
        slots[0][5] = (part + slots[1][1].astype(F32)).astype(BF)
        return a, send(slots[0].at[5], slots[1].at[5], right)

    def total_x(plane, near, joined):
        arrived = b_in.at[plane]
        block = in_vocab(0, plane)
        near[1].wait_recv()
        joined[0].wait_recv()
        a = input_part(block, 0) + arrived[3].astype(F32) + arrived[4].astype(F32)
        near[0].wait_recv()
        joined[1].wait_recv()
        b = input_part(block, HALF) + arrived[2].astype(F32) + arrived[5].astype(F32)
        return a, b

    up, down = at_tok(0, 1, 0), at_tok(0, 3, 0)

    def head_part(chunk):
        def step(i, _):
            two = pl.multiple_of(i * 384, 384)
            for mine, kept, first in (
                (dlog, held, core * (D // 2)),
                (dlog_other, held_other, 0),
            ):
                part = lax.dot_general(
                    mine[pl.ds(two, 384), :],
                    kept[rows(first + chunk * WIDE, WIDE), :],
                    (((1,), (1,)), ((), ())),
                    preferred_element_type=F32,
                ).reshape(2, 4, GROUP, WIDE)
                if kept is held:
                    g_sum[chunk, pl.ds(i * 2, 2)] = part
                else:
                    g_sum[chunk, pl.ds(i * 2, 2)] += part
            return 0

        lax.fori_loop(0, 2, step, 0)

    def far_y(chunk):
        to = (y + 2) % 4
        out, arrives = c_out.at[chunk], c_in.at[chunk]
        out[0] = g_sum[chunk, pl.ds(0, 2), to].astype(BF)
        a = send(out.at[0], arrives.at[0], down)
        out[1] = g_sum[chunk, pl.ds(2, 2), to].astype(BF)
        return a, send(out.at[1], arrives.at[1], up)

    def direct_y(chunk):
        out, arrives = c_out.at[chunk], c_in.at[chunk]
        out[2] = g_sum[chunk, pl.ds(2, 2), (y + 3) % 4].astype(BF)
        b = send(out.at[2], arrives.at[2], down)
        out[3] = g_sum[chunk, pl.ds(0, 2), (y + 1) % 4].astype(BF)
        return b, send(out.at[3], arrives.at[3], up)

    def joined_y(chunk, far):
        out, arrives = c_out.at[chunk], c_in.at[chunk]
        far[0].wait_recv()
        part = g_sum[chunk, pl.ds(0, 2), (y + 3) % 4]
        out[4] = (part + arrives[0].astype(F32)).astype(BF)
        a = send(out.at[4], arrives.at[4], down)
        far[1].wait_recv()
        part = g_sum[chunk, pl.ds(2, 2), (y + 1) % 4]
        out[5] = (part + arrives[1].astype(F32)).astype(BF)
        return a, send(out.at[5], arrives.at[5], up)

    def total_y(chunk, near, joined):
        arrives = c_in.at[chunk]
        near[1].wait_recv()
        joined[0].wait_recv()
        mine = g_sum.at[chunk, pl.ds(0, 2), y]
        mine[...] += arrives[3].astype(F32) + arrives[4].astype(F32)
        near[0].wait_recv()
        joined[1].wait_recv()
        mine = g_sum.at[chunk, pl.ds(2, 2), y]
        mine[...] += arrives[2].astype(F32) + arrives[5].astype(F32)
        copies = []
        for k in range(3):
            to = (z_hi + k + 1) % 4
            c_zout[chunk, k] = g_sum[chunk, to, y].astype(BF)
            copies.append(
                send(c_zout.at[chunk, k], c_zin.at[chunk, k], at_tok(k + 1, 0, 0))
            )
        return copies

    kept_rows = pl.ds(pl.multiple_of(core * 24, 8), 24)
    given_rows = pl.ds(pl.multiple_of((1 - core) * 24, 8), 24)

    def total_z(chunk, copies):
        for copy in copies:
            copy.wait_recv()
        mine = g_sum.at[chunk, z_hi, y]
        whole = mine[...]
        for k in range(3):
            whole += c_zin[chunk, k].astype(F32)
        mine[...] = whole
        last_out[chunk] = mine[given_rows, :]
        copy = send(last_out.at[chunk], last_in.at[chunk], at_tok(0, 0, 1))
        at = pl.multiple_of(core * (D // 2) + chunk * WIDE, 128)
        grad_head[:, pl.ds(at, WIDE)] = mine[kept_rows, :]
        return copy

    far_1 = across_x(1)
    share.wait_recv()
    share_dlog.wait_recv()
    head_part(0)
    far_c0, near_c0 = far_y(0), direct_y(0)
    near_1 = direct_x(1)
    head_part(1)
    far_c1, near_c1 = far_y(1), direct_y(1)
    far_0 = across_x(0)
    head_part(2)
    far_c2, near_c2 = far_y(2), direct_y(2)
    joined_c0 = joined_y(0, far_c0)
    joined_1 = joined_x(1, far_1)
    near_0 = direct_x(0)
    joined_c1 = joined_y(1, far_c1)
    joined_c2 = joined_y(2, far_c2)
    far_z0 = total_y(0, near_c0, joined_c0)
    a, b = total_x(1, near_1, joined_1)
    b_zout[0] = a.astype(BF)
    plane_a = send(b_zout.at[0], b_zin.at[0], pair)
    b_zout[1] = b.astype(BF)
    plane_b = send(b_zout.at[1], b_zin.at[1], pair)
    joined_0 = joined_x(0, far_0)
    far_z1 = total_y(1, near_c1, joined_c1)
    far_z2 = total_y(2, near_c2, joined_c2)
    last = [total_z(0, far_z0), total_z(1, far_z1)]
    a, b = total_x(0, near_0, joined_0)
    plane_a.wait_recv()
    plane_b.wait_recv()
    grad_in[:, pl.ds(0, HALF)] = (a + b_zin[0].astype(F32)).astype(BF).T
    grad_in[:, pl.ds(HALF, HALF)] = (b + b_zin[1].astype(F32)).astype(BF).T
    last.append(total_z(2, far_z2))
    for chunk in range(CHUNKS):
        last[chunk].wait_recv()
        at = pl.multiple_of((1 - core) * (D // 2) + chunk * WIDE, 128)
        grad_head[:, pl.ds(at, WIDE)] = last_in[chunk]
    for copy in started:
        copy.wait_send()


COPIES = 16 + 2 + 7 + 2 * 6 + 2 + CHUNKS * 10


def per_device(hidden, head_weight, targets, loss_grad):
    vmem = pl.BlockSpec(memory_space=pltpu.VMEM)
    grad_in, grad_head, loss = pl.pallas_call(
        body,
        out_shape=(
            jax.ShapeDtypeStruct((TOK, COL), BF),
            jax.ShapeDtypeStruct((24, D), F32),
            jax.ShapeDtypeStruct((1, TOK), F32),
        ),
        in_specs=[vmem, pl.BlockSpec(memory_space=pl.ANY), vmem, vmem],
        out_specs=(vmem, vmem, vmem),
        scratch_shapes=[
            pltpu.VMEM((VOC, D), BF),
            pltpu.VMEM((D, VOC), BF),
            pltpu.VMEM((D, TOK), BF),
            pltpu.VMEM((D // 2, TOK), BF),
            pltpu.VMEM((VOC, TOK), F32),
            pltpu.VMEM((VOC, TOK), BF),
            pltpu.VMEM((VOC, TOK), BF),
            pltpu.VMEM((8, 8, TOK), F32),
            pltpu.VMEM((2, 6, HALF, TOK), BF),
            pltpu.VMEM((2, 6, HALF, TOK), BF),
            pltpu.VMEM((2, HALF, TOK), BF),
            pltpu.VMEM((2, HALF, TOK), BF),
            pltpu.VMEM((CHUNKS, 4, 4, GROUP, WIDE), F32),
            pltpu.VMEM((CHUNKS, 6, 2, GROUP, WIDE), BF),
            pltpu.VMEM((CHUNKS, 6, 2, GROUP, WIDE), BF),
            pltpu.VMEM((CHUNKS, 3, GROUP, WIDE), BF),
            pltpu.VMEM((CHUNKS, 3, GROUP, WIDE), BF),
            pltpu.VMEM((CHUNKS, 24, WIDE), F32),
            pltpu.VMEM((CHUNKS, 24, WIDE), F32),
            pltpu.SemaphoreType.DMA,
            pltpu.SemaphoreType.DMA((COPIES,)),
            pltpu.SemaphoreType.DMA((COPIES,)),
        ],
        compiler_params=pltpu.CompilerParams(
            collective_id=0, has_side_effects=True, vmem_limit_bytes=62 * 2**20
        ),
        name="head_backward",
    )(hidden, head_weight, targets.reshape(1, TOK), loss_grad.reshape(1, TOK))
    return grad_in, grad_head, loss.reshape(TOK)


def solution(mesh):
    in_specs = (P("tok", "vocab"), P("vocab", None), P("tok"), P("tok"))
    out_specs = (P("tok", "vocab"), P(("vocab", "tok"), None), P("tok"))
    return jax.shard_map(
        per_device, mesh=mesh, in_specs=in_specs, out_specs=out_specs, check_vma=False
    )
```

```python
import jax
import jax.numpy as jnp
from jax import lax
from jax.experimental import pallas as pl
from jax.experimental.pallas import tpu as pltpu
from jax.sharding import PartitionSpec as P

MESH = pl.DeviceIdType.MESH
D = 5376
VOC = 768
TOK = 512
COL = 672
PIECE = 112
CHUNKS = 7
DEEP = 3
WIDE = D // 2 // CHUNKS
GROUP = 48
BF = jnp.bfloat16
F32 = jnp.float32


def rows(start, size):
    return pl.ds(pl.multiple_of(start, 16), size)


def body(
    hidden, weight, targets, scales, grad_in, grad_head, loss,
    staged, weight_t, held, held_other, logits, dlog, dlog_other, stats,
    b_out, b_in, b_zout, b_zin, g_sum, c_out, c_in, c_zout, c_zin, last_out, last_in,
    local_sem, send_sem, recv_sem,
):
    vocab = lax.axis_index("vocab")
    tok = lax.axis_index("tok")
    x, z_lo = vocab // 2, vocab % 2
    core, y, z_hi = tok % 2, (tok // 2) % 4, tok // 8

    def in_vocab(dx, dz):
        return ((x + dx) % 4) * 2 + (z_lo + dz) % 2

    def in_tok(dz, dy, dc):
        return (((z_hi + dz) % 4) * 4 + (y + dy) % 4) * 2 + (core + dc) % 2

    def at_vocab(dx, dz):
        return (in_vocab(dx, dz), tok)

    def at_tok(dz, dy, dc):
        return (vocab, in_tok(dz, dy, dc))

    peers = [at_vocab(dx, dz) for dx in range(4) for dz in range(2) if dx or dz]
    others = [at_tok(0, 0, 1), at_tok(0, 1, 0), at_tok(0, 3, 0)]
    others += [at_tok(dz, 0, 0) for dz in (1, 2, 3)]

    barrier = pltpu.get_barrier_semaphore()
    for device in peers + others:
        pl.semaphore_signal(barrier, inc=1, device_id=device, device_id_type=MESH)

    fetch_own = pltpu.make_async_copy(
        hidden, held.at[rows(vocab * COL, COL)], local_sem.at[0]
    )
    fetch_own.start()
    fetch = pltpu.make_async_copy(weight, staged, local_sem.at[1])
    fetch.start()

    started = []
    unsent = {}
    lanes = {}

    def send(src, dst, device, lane=None, most=2):
        at = len(started)
        copy = pltpu.make_async_remote_copy(
            src_ref=src,
            dst_ref=dst,
            send_sem=send_sem.at[at],
            recv_sem=recv_sem.at[at],
            device_id=device,
            device_id_type=MESH,
        )
        if lane is not None:
            queue = lanes.setdefault(lane, [])
            while len(queue) >= most:
                first = queue.pop(0)
                first.wait_send()
                del unsent[id(first)]
            queue.append(copy)
        copy.start()
        started.append(copy)
        unsent[id(copy)] = copy
        return copy

    right, left, pair = at_vocab(1, 0), at_vocab(3, 0), at_vocab(0, 1)
    own = vocab
    from_left, from_right = in_vocab(3, 0), in_vocab(1, 0)
    across, partner = in_vocab(2, 0), in_vocab(0, 1)

    arrival, ready = {}, set()

    def need(key, part):
        if (key, part) not in ready:
            ready.add((key, part))
            arrival[key, part].wait_recv()

    def pass_on(block, part, device, lane, key):
        where = held.at[rows(block * COL + part * PIECE, PIECE)]
        arrival[key, part] = send(where, where, device, lane)

    def own_right(part):
        pass_on(own, part, right, "right", "left")

    def own_left(part):
        pass_on(own, part, left, "left", "right")

    def own_pair(part):
        pass_on(own, part, pair, "pair", "pair")

    def on_right(part):
        need("left", part)
        pass_on(from_left, part, right, "right", "across")

    def on_left(part):
        need("right", part)
        pass_on(from_right, part, left, "left", "across")

    def z_right(part):
        need("pair", part)
        pass_on(partner, part, right, "right", "pair left")

    def z_left(part):
        need("pair", part)
        pass_on(partner, part, left, "left", "pair right")

    def pair_from_right(part):
        need("right", part)
        pass_on(from_right, part, pair, "pair", "pair right")

    def pair_from_left(part):
        need("left", part)
        pass_on(from_left, part, pair, "pair", "pair left")

    def pair_across(part):
        need("across", part)
        pass_on(across, part, pair, "pair", "pair across")

    fetch_own.wait()
    pl.semaphore_wait(barrier, len(peers) + len(others))

    def turn(first, count):
        def step(i, _):
            at = pl.multiple_of((first + i) * 128, 128)
            weight_t[pl.ds(at, 128), :] = staged[:, pl.ds(at, 128)].T
            return 0

        lax.fori_loop(0, count, step, 0)

    def logit_part(block, fresh=False):
        def step(i, _):
            at = pl.multiple_of(i * 256, 256)
            part = lax.dot_general(
                weight_t[rows(block * COL, COL), pl.ds(at, 256)],
                held[rows(block * COL, COL), :],
                (((0,), (0,)), ((), ())),
                preferred_element_type=F32,
            )
            if fresh:
                logits[pl.ds(at, 256), :] = part
            else:
                logits[pl.ds(at, 256), :] += part
            return 0

        lax.fori_loop(0, VOC // 256, step, 0)

    order_right = [(own_right, p) for p in (0, 1, 2)]
    order_right += [(on_right, 0), (own_right, 3), (on_right, 1), (own_right, 4)]
    order_right += [(on_right, 2), (own_right, 5)] + [(z_right, p) for p in range(5)]
    order_left = [(own_left, p) for p in (5, 4, 3)]
    order_left += [(on_left, 5), (own_left, 2), (on_left, 4), (own_left, 1)]
    order_left += [(on_left, 3), (own_left, 0)] + [(z_left, p) for p in range(5)]
    order_pair = [(own_pair, p) for p in range(6)]
    order_pair += [(pair_from_right, 5), (pair_across, 0), (pair_across, 5)]
    order_pair += [(pair_across, 1), (pair_across, 4), (pair_from_left, 5)]
    order_pair += [(pair_across, 2), (pair_across, 3)]
    def whole(key, block, fresh=False):
        for part in range(6):
            need(key, part)
        logit_part(block, fresh)

    for slot in range(14):
        for order in (order_right, order_left, order_pair):
            step, part = order[slot]
            step(part)
        if slot == 1:
            fetch.wait()
        if 1 <= slot <= 7:
            turn(6 * slot - 6, 6)
        if slot == 8:
            logit_part(own, fresh=True)
        if slot == 9:
            whole("pair", partner)
        if slot == 11:
            whole("left", from_left)
        if slot == 12:
            whole("right", from_right)
        if slot == 13:
            whole("across", across)
    whole("pair left", in_vocab(3, 1))
    whole("pair right", in_vocab(1, 1))
    for part in range(6):
        need("pair across", part)
    share = send(
        held.at[rows((1 - core) * (D // 2), D // 2)], held_other, at_tok(0, 0, 1)
    )
    logit_part(in_vocab(2, 1))

    chosen = targets[...] - vocab * VOC
    steps = VOC // 64
    peak = jnp.full((8, TOK), -jnp.inf, F32)

    def find_peak(i, peak):
        part = logits[pl.ds(pl.multiple_of(i * 64, 64), 64), :]
        return jnp.maximum(peak, jnp.max(part.reshape(8, 8, TOK), axis=0))

    peak = lax.fori_loop(0, steps, find_peak, peak)
    peak = jnp.max(peak, axis=0, keepdims=True)
    ids = lax.broadcasted_iota(jnp.int32, (64, TOK), 0)

    def add_up(i, carry):
        total, picked = carry
        at = pl.multiple_of(i * 64, 64)
        part = logits[pl.ds(at, 64), :]
        hit = ids == chosen - at
        picked += jnp.sum(jnp.where(hit, part, 0.0).reshape(8, 8, TOK), axis=0)
        part = jnp.exp(part - peak)
        logits[pl.ds(at, 64), :] = part
        total += jnp.sum(part.reshape(8, 8, TOK), axis=0)
        return total, picked

    zeros = jnp.zeros((8, TOK), F32)
    total, picked = lax.fori_loop(0, steps, add_up, (zeros, zeros))
    total = jnp.sum(total, axis=0, keepdims=True)
    picked = jnp.sum(picked, axis=0, keepdims=True)
    stats[own] = jnp.concatenate([peak, total, picked, zeros[:5]], axis=0)
    told = [send(stats.at[own], stats.at[own], device) for device in peers]
    for copy in told:
        copy.wait_recv()
    heard = stats[...]
    peaks, totals, picks = heard[:, 0, :], heard[:, 1, :], heard[:, 2, :]
    row_peak = jnp.max(peaks, axis=0, keepdims=True)
    row_total = jnp.sum(totals * jnp.exp(peaks - row_peak), axis=0, keepdims=True)
    target_logit = jnp.sum(picks, axis=0, keepdims=True)
    loss[...] = row_peak + jnp.log(row_total) - target_logit
    share_of = jnp.exp(peak - row_peak) / row_total
    scale = scales[...]

    def make_dlog(i, _):
        at = pl.multiple_of(i * 64, 64)
        part = logits[pl.ds(at, 64), :] * share_of
        hit = ids == chosen - at
        part = scale * (part - jnp.where(hit, 1.0, 0.0))
        dlog[pl.ds(at, 64), :] = part.astype(BF)
        return 0

    lax.fori_loop(0, steps, make_dlog, 0)
    share_dlog = send(dlog, dlog_other, at_tok(0, 0, 1))

    def input_part(block, part):
        return jnp.dot(
            weight_t[rows(block * COL + part * PIECE, PIECE), :],
            dlog[...],
            preferred_element_type=F32,
        )

    def to_left(group, slot, part):
        b_out[group, slot] = part.astype(BF)
        return send(
            b_out.at[group, slot], b_in.at[group, slot], left, "left", DEEP
        )

    def to_right(group, slot, part):
        b_out[group, slot] = part.astype(BF)
        return send(
            b_out.at[group, slot], b_in.at[group, slot], right, "right", DEEP
        )

    def arrived(group, slot):
        return b_in[group, slot].astype(F32)

    far_b, near_b, joined_b, plane_b = {}, {}, {}, {}

    def far_x(group):
        block, low = in_vocab(2, 1 - group // 3), group % 3
        a = to_left(group, 0, input_part(block, low))
        far_b[group] = a, to_right(group, 1, input_part(block, low + 3))

    def direct_x(group):
        plane, low = 1 - group // 3, group % 3
        b = to_left(group, 2, input_part(in_vocab(3, plane), low + 3))
        near_b[group] = b, to_right(group, 3, input_part(in_vocab(1, plane), low))

    def joined_x(group):
        plane, low = 1 - group // 3, group % 3
        part = input_part(in_vocab(3, plane), low)
        far_b[group][0].wait_recv()
        a = to_left(group, 4, part + arrived(group, 0))
        part = input_part(in_vocab(1, plane), low + 3)
        far_b[group][1].wait_recv()
        joined_b[group] = a, to_right(group, 5, part + arrived(group, 1))

    def total_x(group):
        plane, low = 1 - group // 3, group % 3
        block = in_vocab(0, plane)
        a, b = input_part(block, low), input_part(block, low + 3)
        near_b[group][1].wait_recv()
        joined_b[group][0].wait_recv()
        a += arrived(group, 3) + arrived(group, 4)
        near_b[group][0].wait_recv()
        joined_b[group][1].wait_recv()
        b += arrived(group, 2) + arrived(group, 5)
        if plane:
            b_zout[low] = a.astype(BF)
            a = send(b_zout.at[low], b_zin.at[low], pair)
            b_zout[low + 3] = b.astype(BF)
            plane_b[low] = a, send(b_zout.at[low + 3], b_zin.at[low + 3], pair)
        else:
            plane_b[low][0].wait_recv()
            a += b_zin[low].astype(F32)
            grad_in[pl.ds(low * PIECE, PIECE), :] = a.astype(BF)
            plane_b[low][1].wait_recv()
            b += b_zin[low + 3].astype(F32)
            grad_in[pl.ds((low + 3) * PIECE, PIECE), :] = b.astype(BF)

    up, down = at_tok(0, 1, 0), at_tok(0, 3, 0)

    def head_part(chunk):
        def step(i, _):
            two = pl.multiple_of(i * 384, 384)
            for mine, kept, first in (
                (dlog, held, core * (D // 2)),
                (dlog_other, held_other, 0),
            ):
                part = lax.dot_general(
                    mine[pl.ds(two, 384), :],
                    kept[rows(first + chunk * WIDE, WIDE), :],
                    (((1,), (1,)), ((), ())),
                    preferred_element_type=F32,
                ).reshape(2, 4, GROUP, WIDE)
                if kept is held:
                    g_sum[chunk, pl.ds(i * 2, 2)] = part
                else:
                    g_sum[chunk, pl.ds(i * 2, 2)] += part
            return 0

        lax.fori_loop(0, 2, step, 0)

    def to_down(chunk, slot, part):
        c_out[chunk, slot] = part.astype(BF)
        return send(
            c_out.at[chunk, slot], c_in.at[chunk, slot], down, "down", DEEP
        )

    def to_up(chunk, slot, part):
        c_out[chunk, slot] = part.astype(BF)
        return send(c_out.at[chunk, slot], c_in.at[chunk, slot], up, "up", DEEP)

    def landed(chunk, slot):
        return c_in[chunk, slot].astype(F32)

    far_c, near_c, joined_c, zs_c, last = {}, {}, {}, {}, {}
    low, high = pl.ds(0, 2), pl.ds(2, 2)

    def far_y(chunk):
        head_part(chunk)
        to = (y + 2) % 4
        a = to_down(chunk, 0, g_sum[chunk, low, to])
        far_c[chunk] = a, to_up(chunk, 1, g_sum[chunk, high, to])

    def direct_y(chunk):
        b = to_down(chunk, 2, g_sum[chunk, high, (y + 3) % 4])
        near_c[chunk] = b, to_up(chunk, 3, g_sum[chunk, low, (y + 1) % 4])

    def joined_y(chunk):
        far_c[chunk][0].wait_recv()
        a = to_down(chunk, 4, g_sum[chunk, low, (y + 3) % 4] + landed(chunk, 0))
        far_c[chunk][1].wait_recv()
        b = to_up(chunk, 5, g_sum[chunk, high, (y + 1) % 4] + landed(chunk, 1))
        joined_c[chunk] = a, b

    def total_y(chunk):
        near_c[chunk][1].wait_recv()
        joined_c[chunk][0].wait_recv()
        g_sum[chunk, low, y] += landed(chunk, 3) + landed(chunk, 4)
        near_c[chunk][0].wait_recv()
        joined_c[chunk][1].wait_recv()
        g_sum[chunk, high, y] += landed(chunk, 2) + landed(chunk, 5)
        copies = []
        for k in range(3):
            to = (z_hi + k + 1) % 4
            c_zout[chunk, k] = g_sum[chunk, to, y].astype(BF)
            copies.append(
                send(c_zout.at[chunk, k], c_zin.at[chunk, k], at_tok(k + 1, 0, 0))
            )
        zs_c[chunk] = copies

    kept_rows = pl.ds(pl.multiple_of(core * 24, 8), 24)
    given_rows = pl.ds(pl.multiple_of((1 - core) * 24, 8), 24)

    def total_z(chunk):
        for copy in zs_c[chunk]:
            copy.wait_recv()
        mine = g_sum.at[chunk, z_hi, y]
        total = mine[...]
        for k in range(3):
            total += c_zin[chunk, k].astype(F32)
        mine[...] = total
        last_out[chunk] = mine[given_rows, :]
        last[chunk] = send(last_out.at[chunk], last_in.at[chunk], at_tok(0, 0, 1))
        at = pl.multiple_of(core * (D // 2) + chunk * WIDE, 128)
        grad_head[:, pl.ds(at, WIDE)] = mine[kept_rows, :]

    plan = []
    for far, direct, joined, total, count, slot in (
        (far_y, direct_y, joined_y, total_y, CHUNKS, 1.55),
        (far_x, direct_x, joined_x, total_x, 6, 2.4),
    ):
        line = [(far, 0)]
        for n in range(count):
            if n + 1 < count:
                line.append((far, n + 1))
            line += [(direct, n), (joined, n)]
        for at, (step, n) in enumerate(line):
            plan.append((max(0, at + 1 - DEEP) * slot, step, n))
            if step is joined:
                plan.append(((at + 1) * slot + 2, total, n))
                if step is joined_y:
                    plan.append(((at + 1) * slot + 17, total_z, n))
    share.wait_recv()
    share_dlog.wait_recv()
    for _, step, n in sorted(plan, key=lambda entry: entry[0]):
        step(n)
    for chunk in range(CHUNKS):
        last[chunk].wait_recv()
        at = pl.multiple_of((1 - core) * (D // 2) + chunk * WIDE, 128)
        grad_head[:, pl.ds(at, WIDE)] = last_in[chunk]
    for copy in unsent.values():
        copy.wait_send()


def hand_over(*refs):
    for k in range(3):
        refs[3 + k][...] = refs[k][...]


COPIES = 42 + 2 + 7 + 6 * 6 + 6 + CHUNKS * 10


def per_device(hidden, head_weight, targets, loss_grad):
    vmem = pl.BlockSpec(memory_space=pltpu.VMEM)
    hbm = pl.BlockSpec(memory_space=pl.ANY)
    grad_in, grad_head, loss = pl.pallas_call(
        body,
        out_shape=(
            jax.ShapeDtypeStruct((COL, TOK), BF),
            jax.ShapeDtypeStruct((24, D), F32),
            jax.ShapeDtypeStruct((1, TOK), F32),
        ),
        in_specs=[hbm, hbm, vmem, vmem],
        out_specs=(vmem, vmem, vmem),
        scratch_shapes=[
            pltpu.VMEM((VOC, D), BF),
            pltpu.VMEM((D, VOC), BF),
            pltpu.VMEM((D, TOK), BF),
            pltpu.VMEM((D // 2, TOK), BF),
            pltpu.VMEM((VOC, TOK), F32),
            pltpu.VMEM((VOC, TOK), BF),
            pltpu.VMEM((VOC, TOK), BF),
            pltpu.VMEM((8, 8, TOK), F32),
            pltpu.VMEM((6, 6, PIECE, TOK), BF),
            pltpu.VMEM((6, 6, PIECE, TOK), BF),
            pltpu.VMEM((6, PIECE, TOK), BF),
            pltpu.VMEM((6, PIECE, TOK), BF),
            pltpu.VMEM((CHUNKS, 4, 4, GROUP, WIDE), F32),
            pltpu.VMEM((CHUNKS, 6, 2, GROUP, WIDE), BF),
            pltpu.VMEM((CHUNKS, 6, 2, GROUP, WIDE), BF),
            pltpu.VMEM((CHUNKS, 3, GROUP, WIDE), BF),
            pltpu.VMEM((CHUNKS, 3, GROUP, WIDE), BF),
            pltpu.VMEM((CHUNKS, 24, WIDE), F32),
            pltpu.VMEM((CHUNKS, 24, WIDE), F32),
            pltpu.SemaphoreType.DMA((2,)),
            pltpu.SemaphoreType.DMA((COPIES,)),
            pltpu.SemaphoreType.DMA((COPIES,)),
        ],
        compiler_params=pltpu.CompilerParams(
            collective_id=0, has_side_effects=True, vmem_limit_bytes=62 * 2**20
        ),
        name="head_backward",
    )(hidden.T, head_weight, targets.reshape(1, TOK), loss_grad.reshape(1, TOK))
    made = (grad_in, grad_head, loss)
    grad_in, grad_head, loss = pl.pallas_call(
        hand_over,
        out_shape=tuple(jax.ShapeDtypeStruct(a.shape, a.dtype) for a in made),
        in_specs=[vmem] * 3,
        out_specs=(vmem,) * 3,
        name="hand_over",
    )(*made)
    return grad_in.T, grad_head, loss.reshape(TOK)


def solution(mesh):
    in_specs = (P("tok", "vocab"), P("vocab", None), P("tok"), P("tok"))
    out_specs = (P("tok", "vocab"), P(("vocab", "tok"), None), P("tok"))
    return jax.shard_map(
        per_device, mesh=mesh, in_specs=in_specs, out_specs=out_specs, check_vma=False
    )
```

```python
import jax
import jax.numpy as jnp
from jax import lax
from jax.experimental import pallas as pl
from jax.experimental.pallas import tpu as pltpu
from jax.sharding import PartitionSpec as P

MESH = pl.DeviceIdType.MESH
D = 5376
VOC = 768
TOK = 512
COL = 672
PIECE = 112
CHUNKS = 7
HALVES = 1
PART = TOK // HALVES
ROWS = 112
LOWS = 336 // ROWS
GROUPS = 2 * HALVES * LOWS
DEEP = 3
RELAYED = 5
WIDE = D // 2 // CHUNKS
GROUP = 48
BF = jnp.bfloat16
F32 = jnp.float32


class Entry:
    def __init__(self, copy, at):
        self.copy, self.at = copy, at


def rows(start, size):
    return pl.ds(pl.multiple_of(start, 16), size)


def body(
    hidden, weight, targets, scales, grad_in, grad_head, loss,
    staged, weight_t, held, held_other, logits, dlog, dlog_other, stats,
    b_out, b_in, b_zout, b_zin, g_sum, c_out, c_in, c_zout, c_zin, last_out, last_in,
    local_sem, send_sem, recv_sem,
):
    vocab = lax.axis_index("vocab")
    tok = lax.axis_index("tok")
    x, z_lo = vocab // 2, vocab % 2
    core, y, z_hi = tok % 2, (tok // 2) % 4, tok // 8

    def in_vocab(dx, dz):
        return ((x + dx) % 4) * 2 + (z_lo + dz) % 2

    def in_tok(dz, dy, dc):
        return (((z_hi + dz + 4) % 4) * 4 + (y + dy) % 4) * 2 + (core + dc) % 2

    def at_vocab(dx, dz):
        return (in_vocab(dx, dz), tok)

    def at_tok(dz, dy, dc):
        return (vocab, in_tok(dz, dy, dc))

    peers = [at_vocab(dx, dz) for dx in range(4) for dz in range(2) if dx or dz]
    others = [at_tok(0, 0, 1), at_tok(0, 1, 0), at_tok(0, 3, 0)]
    others += [at_tok(dz, 0, 0) for dz in (1, 2, 3)]

    barrier = pltpu.get_barrier_semaphore()
    for device in peers + others:
        pl.semaphore_signal(barrier, inc=1, device_id=device, device_id_type=MESH)

    fetch_own = pltpu.make_async_copy(
        hidden, held.at[rows(vocab * COL, COL)], local_sem.at[0]
    )
    fetch_own.start()
    fetch = pltpu.make_async_copy(weight, staged, local_sem.at[1])
    fetch.start()

    spare, used, unsent, lanes = [], [0, 0], [], {}

    def new_arrival():
        used[1] += 1
        return used[1] - 1

    def sent(entry):
        entry.copy.wait_send()
        unsent.remove(entry)
        spare.append(entry.at)

    def send(src, dst, device, into, lane, most):
        queue = lanes.setdefault(lane, [])
        while len(queue) >= most:
            sent(queue.pop(0))
        if not spare:
            spare.append(used[0])
            used[0] += 1
        at = spare.pop()
        copy = pltpu.make_async_remote_copy(
            src_ref=src,
            dst_ref=dst,
            send_sem=send_sem.at[at],
            recv_sem=recv_sem.at[into],
            device_id=device,
            device_id_type=MESH,
        )
        copy.start()
        entry = Entry(copy, at)
        queue.append(entry)
        unsent.append(entry)

    def arrive(ref, at):
        pltpu.make_async_remote_copy(
            src_ref=ref,
            dst_ref=ref,
            send_sem=send_sem.at[0],
            recv_sem=recv_sem.at[at],
            device_id=at_tok(0, 0, 1),
            device_id_type=MESH,
        ).wait_recv()

    right, left, pair = at_vocab(1, 0), at_vocab(3, 0), at_vocab(0, 1)
    own = vocab
    from_left, from_right = in_vocab(3, 0), in_vocab(1, 0)
    across, partner = in_vocab(2, 0), in_vocab(0, 1)

    arrival, ready = {}, set()
    source = {
        "left": from_left,
        "right": from_right,
        "pair": partner,
        "across": across,
        "pair left": in_vocab(3, 1),
        "pair right": in_vocab(1, 1),
        "pair across": in_vocab(2, 1),
    }

    def lanes_of(half):
        return pl.ds(half * PART, PART)

    def spot(block, part, half):
        return held.at[rows(block * COL + part * PIECE, PIECE), lanes_of(half)]

    def together(key):
        return key.startswith("pair ")

    def need(key, part, half):
        if together(key):
            part = 0
        if (key, part, half) not in ready:
            ready.add((key, part, half))
            ref = spot(source[key], part, half)
            if together(key):
                ref = held.at[rows(source[key] * COL, COL), lanes_of(half)]
            arrive(ref, arrival[key, part, half])

    def pass_on(block, part, half, device, lane, key):
        name = key, 0 if together(key) else part, half
        if name not in arrival:
            arrival[name] = new_arrival()
        where = spot(block, part, half)
        send(where, where, device, arrival[name], lane, HALVES + 1)

    def own_right(part, half):
        pass_on(own, part, half, right, "right", "left")

    def own_left(part, half):
        pass_on(own, part, half, left, "left", "right")

    def own_pair(part, half):
        pass_on(own, part, half, pair, "pair", "pair")

    def on_right(part, half):
        need("left", part, half)
        pass_on(from_left, part, half, right, "right", "across")

    def on_left(part, half):
        need("right", part, half)
        pass_on(from_right, part, half, left, "left", "across")

    def z_right(part, half):
        need("pair", part, half)
        pass_on(partner, part, half, right, "right", "pair left")

    def z_left(part, half):
        need("pair", part, half)
        pass_on(partner, part, half, left, "left", "pair right")

    def pair_from_right(part, half):
        need("right", part, half)
        pass_on(from_right, part, half, pair, "pair", "pair right")

    def pair_from_left(part, half):
        need("left", part, half)
        pass_on(from_left, part, half, pair, "pair", "pair left")

    def pair_across(part, half):
        need("across", part, half)
        pass_on(across, part, half, pair, "pair", "pair across")

    fetch_own.wait()
    pl.semaphore_wait(barrier, len(peers) + len(others))

    def turn(first, count):
        def step(i, _):
            at = pl.multiple_of((first + i) * 128, 128)
            weight_t[pl.ds(at, 128), :] = staged[:, pl.ds(at, 128)].T
            return 0

        lax.fori_loop(0, count, step, 0)

    def logit_range(start, size, half, fresh=False):
        tokens = lanes_of(half)
        start = pl.multiple_of(start, 128)

        def step(i, _):
            at = pl.multiple_of(i * 384, 384)
            part = jnp.dot(
                staged[pl.ds(at, 384), pl.ds(start, size)],
                held[pl.ds(start, size), tokens],
                preferred_element_type=F32,
            )
            if fresh:
                logits[pl.ds(at, 384), tokens] = part
            else:
                logits[pl.ds(at, 384), tokens] += part
            return 0

        lax.fori_loop(0, VOC // 384, step, 0)

    def logit_part(block, half, fresh=False):
        quad, rest = block // 4, block % 4
        logit_range(quad * 2688 + rest * 704 + (rest % 2) * 64, 512, half, fresh)

    def logit_rest(half):
        for start, size in ((512, 256), (1280, 128), (1920, 256)):
            logit_range(start, size, half)
            logit_range(2688 + start, size, half)

    def whole(key, block, half):
        for part in range(6):
            need(key, part, half)
        logit_part(block, half)

    shares = []

    def give_share(half):
        shares.append((held_other.at[:, lanes_of(half)], new_arrival()))
        mine = held.at[rows((1 - core) * (D // 2), D // 2), lanes_of(half)]
        send(mine, *shares[-1][:1], at_tok(0, 0, 1), shares[-1][1], "core", 2)

    steps = VOC // 64
    ids = lax.broadcasted_iota(jnp.int32, (64, PART), 0)
    zeros = jnp.zeros((8, PART), F32)
    peak_of, chosen_of, told_of = {}, {}, {}

    def local_softmax(half):
        tokens = lanes_of(half)
        chosen = targets[:, tokens] - vocab * VOC

        def find_peak(i, peak):
            part = logits[pl.ds(pl.multiple_of(i * 64, 64), 64), tokens]
            return jnp.maximum(peak, jnp.max(part.reshape(8, 8, PART), axis=0))

        peak = jnp.full((8, PART), -jnp.inf, F32)
        peak = lax.fori_loop(0, steps, find_peak, peak)
        peak = jnp.max(peak, axis=0, keepdims=True)

        def add_up(i, carry):
            total, picked = carry
            at = pl.multiple_of(i * 64, 64)
            part = logits[pl.ds(at, 64), tokens]
            hit = ids == chosen - at
            picked += jnp.sum(jnp.where(hit, part, 0.0).reshape(8, 8, PART), axis=0)
            part = jnp.exp(part - peak)
            logits[pl.ds(at, 64), tokens] = part
            total += jnp.sum(part.reshape(8, 8, PART), axis=0)
            return total, picked

        total, picked = lax.fori_loop(0, steps, add_up, (zeros, zeros))
        total = jnp.sum(total, axis=0, keepdims=True)
        picked = jnp.sum(picked, axis=0, keepdims=True)
        stats[half, own] = jnp.concatenate([peak, total, picked, zeros[:5]], axis=0)
        where = stats.at[half, own]
        told_of[half] = new_arrival()
        for device in peers:
            send(where, where, device, told_of[half], "stats", 7)
        peak_of[half], chosen_of[half] = peak, chosen

    def full_softmax(half):
        tokens = lanes_of(half)
        arrive(stats.at[half, pl.ds(0, 7)], told_of[half])
        heard = stats[half]
        peaks, totals, picks = heard[:, 0, :], heard[:, 1, :], heard[:, 2, :]
        row_peak = jnp.max(peaks, axis=0, keepdims=True)
        row_total = jnp.sum(totals * jnp.exp(peaks - row_peak), axis=0, keepdims=True)
        target_logit = jnp.sum(picks, axis=0, keepdims=True)
        loss[:, tokens] = row_peak + jnp.log(row_total) - target_logit
        share_of = jnp.exp(peak_of[half] - row_peak) / row_total
        scale, chosen = scales[:, tokens], chosen_of[half]

        def make_dlog(i, _):
            at = pl.multiple_of(i * 64, 64)
            part = logits[pl.ds(at, 64), tokens] * share_of
            hit = ids == chosen - at
            part = scale * (part - jnp.where(hit, 1.0, 0.0))
            dlog[pl.ds(at, 64), tokens] = part.astype(BF)
            return 0

        lax.fori_loop(0, steps, make_dlog, 0)
        shares.append((dlog_other.at[:, tokens], new_arrival()))
        send(dlog.at[:, tokens], *shares[-1][:1], at_tok(0, 0, 1), shares[-1][1], "core", 2)

    order_right = [(own_right, p) for p in (0, 1, 2)]
    order_right += [(on_right, 0), (own_right, 3), (on_right, 1), (own_right, 4)]
    order_right += [(on_right, 2), (own_right, 5)] + [(z_right, p) for p in range(5)]
    order_left = [(own_left, p) for p in (5, 4, 3)]
    order_left += [(on_left, 5), (own_left, 2), (on_left, 4), (own_left, 1)]
    order_left += [(on_left, 3), (own_left, 0)] + [(z_left, p) for p in range(5)]
    order_pair = [(own_pair, p) for p in range(6)]
    order_pair += [(pair_from_right, 5), (pair_across, 0), (pair_across, 5)]
    order_pair += [(pair_across, 1), (pair_across, 4), (pair_from_left, 5)]
    order_pair += [(pair_across, 2), (pair_across, 3)]

    def work(slot, half):
        if slot == 1 and half == 0:
            fetch.wait()
        if 1 <= slot <= 7 and half == 0:
            turn(6 * slot - 6, 6)
        if slot == 8:
            logit_part(own, half, fresh=True)
        if slot == 10:
            whole("pair", partner, half)
        if slot == 12:
            whole("left", from_left, half)
        if slot == 13:
            whole("right", from_right, half)
        if slot == 14:
            whole("across", across, half)
        if slot == 16:
            whole("pair left", in_vocab(3, 1), half)
        if slot == 17:
            whole("pair right", in_vocab(1, 1), half)
        if slot == 18:
            whole("pair across", in_vocab(2, 1), half)
            give_share(half)
            logit_rest(half)
        if slot == 19:
            local_softmax(half)
        if slot == 23:
            full_softmax(half)

    for slot in range(14 * HALVES):
        for order in (order_right, order_left, order_pair):
            step, part = order[slot % 14]
            step(part, slot // 14)
        for half in range(HALVES):
            work(slot - 14 * half, half)

    def input_part(block, part, half):
        return jnp.dot(
            weight_t[rows(block * COL + part * ROWS, ROWS), :],
            dlog[:, lanes_of(half)],
            preferred_element_type=F32,
        )

    def to_x(device, lane, group, slot, part):
        b_out[group, slot] = part.astype(BF)
        where = b_out.at[group, slot], b_in.at[group, slot]
        send(*where, device, arrive_b[group][slot // 2 > 0], lane, DEEP)

    def to_left(group, slot, part):
        to_x(left, "left", group, slot, part)

    def to_right(group, slot, part):
        to_x(right, "right", group, slot, part)

    def arrived(group, slot):
        return b_in[group, slot].astype(F32)

    arrive_b, plane_b = {}, {}

    def place(group):
        half, rest = group // (2 * LOWS), group % (2 * LOWS)
        return half, 1 - rest // LOWS, rest % LOWS

    def far_x(group):
        arrive_b[group] = new_arrival(), new_arrival()
        half, plane, low = place(group)
        block = in_vocab(2, plane)
        to_left(group, 0, input_part(block, low, half))
        to_right(group, 1, input_part(block, low + LOWS, half))

    def direct_x(group):
        half, plane, low = place(group)
        to_left(group, 2, input_part(in_vocab(3, plane), low + LOWS, half))
        to_right(group, 3, input_part(in_vocab(1, plane), low, half))

    def joined_x(group):
        half, plane, low = place(group)
        a = input_part(in_vocab(3, plane), low, half)
        b = input_part(in_vocab(1, plane), low + LOWS, half)
        arrive(b_in.at[group, pl.ds(0, 2)], arrive_b[group][0])
        to_left(group, 4, a + arrived(group, 0))
        to_right(group, 5, b + arrived(group, 1))

    def total_x(group):
        half, plane, low = place(group)
        block = in_vocab(0, plane)
        a = input_part(block, low, half)
        b = input_part(block, low + LOWS, half)
        arrive(b_in.at[group, pl.ds(2, 4)], arrive_b[group][1])
        a += arrived(group, 3) + arrived(group, 4)
        b += arrived(group, 2) + arrived(group, 5)
        if plane:
            plane_b[half, low] = new_arrival()
            for k, part in enumerate((a, b)):
                b_zout[half, low, k] = part.astype(BF)
                where = b_zout.at[half, low, k], b_zin.at[half, low, k]
                send(*where, pair, plane_b[half, low], "pair", 4)
        else:
            tokens = lanes_of(half)
            arrive(b_zin.at[half, low], plane_b[half, low])
            a += b_zin[half, low, 0].astype(F32)
            grad_in[pl.ds(low * ROWS, ROWS), tokens] = a.astype(BF)
            b += b_zin[half, low, 1].astype(F32)
            grad_in[pl.ds((low + LOWS) * ROWS, ROWS), tokens] = b.astype(BF)

    up, down = at_tok(0, 1, 0), at_tok(0, 3, 0)

    def head_part(chunk):
        def step(i, _):
            two = pl.multiple_of(i * 768, 768)
            for mine, kept, first in (
                (dlog, held, core * (D // 2)),
                (dlog_other, held_other, 0),
            ):
                part = lax.dot_general(
                    mine[pl.ds(two, 768), :],
                    kept[rows(first + chunk * WIDE, WIDE), :],
                    (((1,), (1,)), ((), ())),
                    preferred_element_type=F32,
                ).reshape(4, 4, GROUP, WIDE)
                if kept is held:
                    g_sum[chunk] = part
                else:
                    g_sum[chunk] += part
            return 0

        lax.fori_loop(0, 1, step, 0)

    def to_y(device, lane, chunk, slot, part):
        c_out[chunk, slot] = part.astype(BF)
        where = c_out.at[chunk, slot], c_in.at[chunk, slot]
        send(*where, device, arrive_c[chunk][slot // 2 > 0], lane, DEEP)

    def to_down(chunk, slot, part):
        to_y(down, "down", chunk, slot, part)

    def to_up(chunk, slot, part):
        to_y(up, "up", chunk, slot, part)

    def landed(chunk, slot):
        return c_in[chunk, slot].astype(F32)

    arrive_c, arrive_z, arrive_last = {}, {}, new_arrival()
    low, high = pl.ds(0, 2), pl.ds(2, 2)

    def far_y(chunk):
        arrive_c[chunk] = new_arrival(), new_arrival()
        if chunk == 0:
            for shared in shares:
                arrive(*shared)
        head_part(chunk)
        to = (y + 2) % 4
        to_down(chunk, 0, g_sum[chunk, low, to])
        to_up(chunk, 1, g_sum[chunk, high, to])

    def direct_y(chunk):
        to_down(chunk, 2, g_sum[chunk, high, (y + 3) % 4])
        to_up(chunk, 3, g_sum[chunk, low, (y + 1) % 4])

    def joined_y(chunk):
        arrive(c_in.at[chunk, pl.ds(0, 2)], arrive_c[chunk][0])
        to_down(chunk, 4, g_sum[chunk, low, (y + 3) % 4] + landed(chunk, 0))
        to_up(chunk, 5, g_sum[chunk, high, (y + 1) % 4] + landed(chunk, 1))

    def total_y(chunk):
        arrive(c_in.at[chunk, pl.ds(2, 4)], arrive_c[chunk][1])
        g_sum[chunk, low, y] += landed(chunk, 3) + landed(chunk, 4)
        g_sum[chunk, high, y] += landed(chunk, 2) + landed(chunk, 5)
        arrive_z[chunk] = new_arrival(), new_arrival()
        turn_z = 1 - 2 * (chunk % 2)
        to_z(chunk, 0, turn_z * (1 + (chunk >= RELAYED)), g_sum[chunk, (z_hi + 2) % 4, y])
        to_z(chunk, 1, -turn_z, g_sum[chunk, (z_hi - turn_z + 4) % 4, y])
        if chunk >= RELAYED:
            to_z(chunk, 2, turn_z, g_sum[chunk, (z_hi + turn_z + 4) % 4, y])

    def to_z(chunk, slot, by, part):
        c_zout[chunk, slot] = part.astype(BF)
        where = c_zout.at[chunk, slot], c_zin.at[chunk, slot]
        send(*where, at_tok(by, 0, 0), arrive_z[chunk][slot > 0], "z", 9)

    def joined_z(chunk):
        if chunk >= RELAYED:
            return
        turn_z = 1 - 2 * (chunk % 2)
        arrive(c_zin.at[chunk, 0], arrive_z[chunk][0])
        part = g_sum[chunk, (z_hi + turn_z + 4) % 4, y]
        to_z(chunk, 2, turn_z, part + c_zin[chunk, 0].astype(F32))

    kept_rows = pl.ds(pl.multiple_of(core * 24, 8), 24)
    given_rows = pl.ds(pl.multiple_of((1 - core) * 24, 8), 24)

    def total_z(chunk):
        if chunk >= RELAYED:
            arrive(c_zin.at[chunk, 0], arrive_z[chunk][0])
        arrive(c_zin.at[chunk, pl.ds(1, 2)], arrive_z[chunk][1])
        mine = g_sum.at[chunk, z_hi, y]
        total = mine[...] + c_zin[chunk, 1].astype(F32) + c_zin[chunk, 2].astype(F32)
        if chunk >= RELAYED:
            total += c_zin[chunk, 0].astype(F32)
        mine[...] = total
        last_out[chunk] = mine[given_rows, :]
        where = last_out.at[chunk], last_in.at[chunk]
        send(*where, at_tok(0, 0, 1), arrive_last, "core", 8)
        at = pl.multiple_of(core * (D // 2) + chunk * WIDE, 128)
        grad_head[:, pl.ds(at, WIDE)] = mine[kept_rows, :]

    plan = []
    for slot in range(14, 24):
        work(slot, HALVES - 1)
    for far, direct, joined, total, count, slot in (
        (far_x, direct_x, joined_x, total_x, GROUPS, 14.5 / GROUPS),
        (far_y, direct_y, joined_y, total_y, CHUNKS, 1.55),
    ):
        line = [(far, 0), (direct, 0)]
        for n in range(count):
            if n + 1 < count:
                line += [(far, n + 1), (joined, n), (direct, n + 1)]
            else:
                line.append((joined, n))
        for at, (step, n) in enumerate(line):
            plan.append((max(at * 0.01, (at + 1 - DEEP) * slot), step, n))
            if step is joined:
                plan.append(((at + 1) * slot + 2, total, n))
                if step is joined_y:
                    plan.append(((at + 1) * slot + 6, joined_z, n))
                    plan.append(((at + 1) * slot + 17, total_z, n))
    for _, step, n in sorted(plan, key=lambda entry: entry[0]):
        step(n)
    arrive(last_in, arrive_last)
    for chunk in range(CHUNKS):
        at = pl.multiple_of((1 - core) * (D // 2) + chunk * WIDE, 128)
        grad_head[:, pl.ds(at, WIDE)] = last_in[chunk]
    for entry in list(unsent):
        sent(entry)
    assert used[0] <= SENDS and used[1] <= ARRIVALS


def hand_over(*refs):
    for k in range(3):
        refs[3 + k][...] = refs[k][...]


SENDS, ARRIVALS = 40, 74


def per_device(hidden, head_weight, targets, loss_grad):
    vmem = pl.BlockSpec(memory_space=pltpu.VMEM)
    hbm = pl.BlockSpec(memory_space=pl.ANY)
    grad_in, grad_head, loss = pl.pallas_call(
        body,
        out_shape=(
            jax.ShapeDtypeStruct((COL, TOK), BF),
            jax.ShapeDtypeStruct((24, D), F32),
            jax.ShapeDtypeStruct((1, TOK), F32),
        ),
        in_specs=[hbm, hbm, vmem, vmem],
        out_specs=(vmem, vmem, vmem),
        scratch_shapes=[
            pltpu.VMEM((VOC, D), BF),
            pltpu.VMEM((D, VOC), BF),
            pltpu.VMEM((D, TOK), BF),
            pltpu.VMEM((D // 2, TOK), BF),
            pltpu.VMEM((VOC, TOK), F32),
            pltpu.VMEM((VOC, TOK), BF),
            pltpu.VMEM((VOC, TOK), BF),
            pltpu.VMEM((HALVES, 8, 8, PART), F32),
            pltpu.VMEM((GROUPS, 6, ROWS, PART), BF),
            pltpu.VMEM((GROUPS, 6, ROWS, PART), BF),
            pltpu.VMEM((HALVES, LOWS, 2, ROWS, PART), BF),
            pltpu.VMEM((HALVES, LOWS, 2, ROWS, PART), BF),
            pltpu.VMEM((CHUNKS, 4, 4, GROUP, WIDE), F32),
            pltpu.VMEM((CHUNKS, 6, 2, GROUP, WIDE), BF),
            pltpu.VMEM((CHUNKS, 6, 2, GROUP, WIDE), BF),
            pltpu.VMEM((CHUNKS, 3, GROUP, WIDE), BF),
            pltpu.VMEM((CHUNKS, 3, GROUP, WIDE), BF),
            pltpu.VMEM((CHUNKS, 24, WIDE), F32),
            pltpu.VMEM((CHUNKS, 24, WIDE), F32),
            pltpu.SemaphoreType.DMA((2,)),
            pltpu.SemaphoreType.DMA((SENDS,)),
            pltpu.SemaphoreType.DMA((ARRIVALS,)),
        ],
        compiler_params=pltpu.CompilerParams(
            collective_id=0, has_side_effects=True, vmem_limit_bytes=62 * 2**20
        ),
        name="head_backward",
    )(hidden.T, head_weight, targets.reshape(1, TOK), loss_grad.reshape(1, TOK))
    made = (grad_in, grad_head, loss)
    grad_in, grad_head, loss = pl.pallas_call(
        hand_over,
        out_shape=tuple(jax.ShapeDtypeStruct(a.shape, a.dtype) for a in made),
        in_specs=[vmem] * 3,
        out_specs=(vmem,) * 3,
        name="hand_over",
    )(*made)
    return grad_in.T, grad_head, loss.reshape(TOK)


def solution(mesh):
    in_specs = (P("tok", "vocab"), P("vocab", None), P("tok"), P("tok"))
    out_specs = (P("tok", "vocab"), P(("vocab", "tok"), None), P("tok"))
    return jax.shard_map(
        per_device, mesh=mesh, in_specs=in_specs, out_specs=out_specs, check_vma=False
    )
```
